256 devices in a mesh: section: 8 (over z), shard: 32 (over y, x, core).
Axes of the slice: x: 4, y: 4, z: 8, core: 2. Of those that a mesh axis runs over, the one named last changes fastest.
Arguments:
- tokens: bfloat16 [4, 64, 8192], P(None, 'shard'), may hold values from -6 to 6
- lengths: int32 [4], replicated, may hold values from 1 to 64, 160 in all
- norm_gain: float32 [8, 8192], P('section'), may hold values from 0.25 to 1.75
- gate_tiles: bfloat16 [8, 128, 28, 128, 128], P('section', 'shard'), may hold values from -0.09375 to 0.09375
- up_tiles: bfloat16 [8, 128, 28, 128, 128], P('section', 'shard'), may hold values from -0.09375 to 0.09375
- in_index: int32 [8, 128, 28], P('section', 'shard'), may hold values from -1 to 63, as said below
- down_tiles: bfloat16 [8, 128, 28, 128, 128], P('section', 'shard'), may hold values from -0.0625 to 0.0625
- out_index: int32 [8, 128, 28], P('section', 'shard'), may hold values from -1 to 63, as said below
Outputs:
- hidden_states: bfloat16 [8, 4, 64, 8192], P('section', None, 'shard')
The draws below stay inside these ranges and needn't reach their ends.
Inputs may be any that keep to these rules, and one draw needn't show every extreme that they name: `in_index`: each list of 28 slots holds distinct block numbers first and -1 in the slots after them; at least 21 slots of every list hold a block number, and in each layer some list holds 28. `out_index`: each list of 28 slots holds distinct block numbers first and -1 in the slots after them; at least 21 slots of every list hold a block number, and in each layer some list holds 28.
All inputs are finite; a program needn't handle non-finite values.
Results may differ from the reference program's by a relative error of at most 0.035.
Values may be sent and summed in bfloat16 or wider, within the bound.
A program may use at most 128 MiB of HBM per device.

```python
import math
import jax
import jax.numpy as jnp
import numpy as np
from jax import lax

D = 8192
FF = 16384
BLOCK = 128
KMAX = 28
MICRO = 4
NB = 64
FF_BLOCKS = 128
HB = 4
LAYERS = 8
ROWS_MB = 64
TOTAL_LIVE = 160
N_SHARD = 32


def block_lists(key):
    key_order, key_count, key_full = jax.random.split(key, 3)
    scores = jax.random.randint(key_order, (LAYERS, FF_BLOCKS, NB), 0, 1 << 20) * NB + jnp.arange(NB, dtype=jnp.int32)
    order = jnp.argsort(scores, axis=-1)[..., :KMAX].astype(jnp.int32)
    counts = jax.random.randint(key_count, (LAYERS, FF_BLOCKS), KMAX - KMAX // 4, KMAX + 1)
    full_group = jax.random.randint(key_full, (LAYERS,), 0, FF_BLOCKS)
    counts = jnp.where(jnp.arange(FF_BLOCKS)[None, :] == full_group[:, None], KMAX, counts)
    slot_ids = jnp.arange(KMAX, dtype=jnp.int32)
    return jnp.where(slot_ids[None, None, :] < counts[:, :, None], order, -1).astype(jnp.int32)


def draw_in_index(key, part):
    return block_lists(jax.random.fold_in(key, 11))


def draw_out_index(key, part):
    return block_lists(jax.random.fold_in(key, 23))


def block_levels(own_key, shape, cuts, low, high):
    gain, own = 1.0, jax.random.fold_in(own_key, 6)
    for axis_at, blocks in cuts:
        draws = jnp.exp(jax.random.uniform(jax.random.fold_in(own, axis_at), (blocks,), jnp.float32, low / len(cuts), high / len(cuts)))
        gain = gain * jnp.repeat(draws, shape[axis_at] // blocks).reshape([-1 if axis == axis_at else 1 for axis in range(len(shape))])
    return gain


def split_up(count, total, most, lean):
    portions = [(1 << 20) // math.isqrt(standing ** lean) + 1 for standing in range(2, count + 1)]
    spare, holding = total - most - (count - 1), [1] * (count - 1)
    while spare > 0:
        candidates = [i for i in range(count - 1) if holding[i] < most]
        pool, budget = sum([portions[i] for i in candidates]), spare
        for i in candidates:
            addition = min(most - holding[i], max(1, budget * portions[i] // pool), spare)
            holding[i] = holding[i] + addition
            spare = spare - addition
    return np.array([most] + holding)


def ragged_sizes(own_key, count, total, bound, slope):
    if count == 2:
        one = jax.random.randint(own_key, (), max(1, total - bound), min(bound, total - 1) + 1)
        return jnp.stack([one, total - one])
    sizes = jnp.asarray(split_up(count, total, bound, slope), jnp.int32)
    twos = (count - 1) // 2
    source_of, receiver = sizes[1:1 + 2 * twos:2], sizes[2:2 + 2 * twos:2]
    slack = jnp.minimum(source_of - 1, bound - receiver)
    shifted = jax.random.randint(jax.random.fold_in(own_key, 1), (twos,), 0, 1 << 20) % (slack + 1)
    sizes = sizes.at[1:1 + 2 * twos:2].set(source_of - shifted).at[2:2 + 2 * twos:2].set(receiver + shifted)
    return sizes[jax.random.permutation(jax.random.fold_in(own_key, 2), count)]


def gaussian(stream_key, shape, scale, reach, cuts=(), kind=jnp.bfloat16):
    array = scale * jax.random.normal(stream_key, shape, jnp.float32)
    if cuts:
        array = array * block_levels(stream_key, shape, cuts, -0.22, 0.18)
    return jnp.clip(array, -reach, reach).astype(kind)


def setup_inputs(seed: int = 0) -> dict:
    arg_keys = jax.random.split(jax.random.key(seed), 9)
    tokens = gaussian(arg_keys[0], (MICRO, ROWS_MB, D), 1.0, 6.0, ((1, 32),))
    lengths = ragged_sizes(arg_keys[1], MICRO, TOTAL_LIVE, ROWS_MB, 1).astype(jnp.int32)
    norm_gain = jnp.clip(1.0 + 0.15 * jax.random.normal(arg_keys[2], (LAYERS, D), jnp.float32), 0.25, 1.75)
    gate_tiles = gaussian(arg_keys[3], (LAYERS, FF_BLOCKS, KMAX, BLOCK, BLOCK), (KMAX * BLOCK) ** -0.5, 0.09375, ((0, 8), (1, 32)))
    up_tiles = gaussian(arg_keys[4], (LAYERS, FF_BLOCKS, KMAX, BLOCK, BLOCK), (KMAX * BLOCK) ** -0.5, 0.09375, ((0, 8), (1, 32)))
    in_index = draw_in_index(jax.random.fold_in(arg_keys[8], 71), 0)
    down_tiles = gaussian(arg_keys[6], (LAYERS, FF_BLOCKS, KMAX, BLOCK, BLOCK), (FF * KMAX // NB) ** -0.5, 0.0625, ((0, 8), (1, 32)))
    out_index = draw_out_index(jax.random.fold_in(arg_keys[8], 71), 0)
    return {"tokens": tokens, "lengths": lengths, "norm_gain": norm_gain, "gate_tiles": gate_tiles, "up_tiles": up_tiles, "in_index": in_index, "down_tiles": down_tiles, "out_index": out_index}


norm_eps = 1e-05

def group_terms(normed, gate_group, up_group, in_group, down_group, out_group):
    row_count = normed.shape[0]
    column_blocks = normed.reshape(row_count, NB, BLOCK)
    in_valid = (in_group >= 0).astype(jnp.bfloat16)
    picked = jnp.take(column_blocks, jnp.maximum(in_group, 0).astype(jnp.int32), axis=1)
    picked = picked * in_valid[None, :, :, None]
    picked = picked.astype(jnp.float32)
    gate_val = jnp.einsum('nhkc,hkcf->nhf', picked, gate_group.astype(jnp.float32), precision=lax.Precision.HIGHEST)
    up_val = jnp.einsum('nhkc,hkcf->nhf', picked, up_group.astype(jnp.float32), precision=lax.Precision.HIGHEST)
    hidden = (jax.nn.silu(gate_val) * up_val).astype(jnp.bfloat16)
    part_terms = jnp.einsum('nhc,hkcf->nhkf', hidden.astype(jnp.float32), down_group.astype(jnp.float32), precision=lax.Precision.HIGHEST)
    onehot = (out_group[:, :, None] == jnp.arange(NB, dtype=jnp.int32)[None, None, :]).astype(jnp.float32)
    placed = jnp.einsum('nhkf,hkb->nbf', part_terms, onehot, precision=lax.Precision.HIGHEST)
    return placed.reshape(row_count, D).astype(jnp.bfloat16)

def layer_apply(arrived, keep_row, gain_row, gate_layer, up_layer, in_layer, down_layer, out_layer):
    widened = arrived.astype(jnp.float32)
    scale_row = lax.rsqrt(lax.optimization_barrier(jnp.mean(widened * widened, axis=-1, keepdims=True)) + norm_eps)
    normed = (widened * scale_row * gain_row[None, :]).astype(jnp.bfloat16)
    grouped = (gate_layer.reshape(N_SHARD, HB, KMAX, BLOCK, BLOCK), up_layer.reshape(N_SHARD, HB, KMAX, BLOCK, BLOCK), in_layer.reshape(N_SHARD, HB, KMAX), down_layer.reshape(N_SHARD, HB, KMAX, BLOCK, BLOCK), out_layer.reshape(N_SHARD, HB, KMAX))

    def accumulate(summed, group):
        term = group_terms(normed, group[0], group[1], group[2], group[3], group[4])
        return (summed + term.astype(jnp.float32), None)
    summed, _ = lax.scan(accumulate, jnp.zeros(widened.shape, jnp.float32), grouped)
    return jnp.where(keep_row[:, None], widened + summed, jnp.float32(0.0)).astype(jnp.bfloat16)

def reference(tokens, lengths, norm_gain, gate_tiles, up_tiles, in_index, down_tiles, out_index):
    row_ids = jnp.arange(ROWS_MB, dtype=jnp.int32)
    keep_all = (row_ids[None, :] < lengths[:, None]).reshape(MICRO * ROWS_MB)
    current = tokens.reshape(MICRO * ROWS_MB, D)
    results = []
    for layer_id in range(LAYERS):
        current = layer_apply(current, keep_all, norm_gain[layer_id], gate_tiles[layer_id], up_tiles[layer_id], in_index[layer_id], down_tiles[layer_id], out_index[layer_id])
        results.append(current.reshape(MICRO, ROWS_MB, D))
    return jnp.stack(results, axis=0)
```

```python
import functools

import jax
import jax.numpy as jnp
from jax import lax
from jax.experimental import pallas as pl
from jax.experimental.pallas import tpu as pltpu
from jax.sharding import PartitionSpec as P

NORM_EPS = 1e-05
LIVE = 160
ROWS = 16
UNITS = LIVE // ROWS
SIDE = 4
CHIPS = SIDE * SIDE
SECTIONS = 8
BLOCK = 128
NB = 64
HALF = NB // 2
HB = 4
KMAX = 28
MESH = pl.DeviceIdType.MESH
SEND_ORDER = sorted(range(CHIPS), key=lambda step: -sum(min(d, SIDE - d) for d in divmod(step, SIDE)))


def kernel(
    lengths, in_index, inverse, tokens, gain, gate, up, down, out,
    gate_up, down_tiles, down_dense, gathered, normed, given, kept, core_got, summed, got, first, result,
    row_send, row_got, out_send, out_got,
    load_sem, gather_sem, gather_sent, core_sem, core_sent, pair_sem, pair_sent,
    scatter_sem, scatter_sent, first_sent, row_sem, row_sent, out_sem, out_sent,
):
    section = lax.axis_index("section")
    shard = lax.axis_index("shard")
    chip = shard // 2
    core = shard % 2
    chip_y = chip // SIDE
    chip_x = chip % SIDE
    half = core * HALF
    other_half = HALF - half
    own = half + chip * 2
    partner = (section, chip * 2 + 1 - core)

    loads = []
    for j in range(HB):
        loads.append(pltpu.make_async_copy(gate.at[j], gate_up.at[j, :, pl.ds(0, BLOCK)], load_sem.at[0, j]))
        loads.append(pltpu.make_async_copy(up.at[j], gate_up.at[j, :, pl.ds(BLOCK, BLOCK)], load_sem.at[1, j]))
        loads.append(pltpu.make_async_copy(down.at[j], down_tiles.at[j, pl.ds(0, KMAX)], load_sem.at[2, j]))
    for load in loads:
        load.start()

    def chip_at(step):
        return (chip_y + step // SIDE) % SIDE * SIDE + (chip_x + step % SIDE) % SIDE

    barrier = pltpu.get_barrier_semaphore()
    before = (section + SECTIONS - 1) % SECTIONS

    def greet_plane(step, carry):
        pl.semaphore_signal(barrier, inc=1, device_id=(section, (shard + step) % 32), device_id_type=MESH)
        return carry

    def greet_before(step, carry):
        pl.semaphore_signal(barrier, inc=1, device_id=(before, step * 2 + core), device_id_type=MESH)
        return carry

    lax.fori_loop(1, 32, greet_plane, 0)
    lax.fori_loop(0, CHIPS, greet_before, 0)
    pl.semaphore_wait(barrier, 31 + CHIPS)

    offsets = [jnp.int32(0)]
    for m in range(3):
        offsets.append(offsets[-1] + lengths[m])

    def position(index):
        block = (index >> 3) & 1
        micro = (index >> 1) & 3
        row = (index >> 4) * 2 + (index & 1)
        start = jnp.full_like(index, 0)
        length = jnp.full_like(index, lengths[0])
        for m in range(1, 4):
            start = jnp.where(micro == m, offsets[m], start)
            length = jnp.where(micro == m, lengths[m], length)
        return jnp.where(row < length, start + row, -1), block

    @pl.when(section == 0)
    def _():
        for b in range(NB):
            owner = b % HALF // 2 * 2 + b // HALF
            row_send[owner, pl.ds(b % 2 * 8, 8), :] = tokens[:, pl.ds(b * BLOCK, BLOCK)]
        pltpu.make_async_copy(row_send.at[shard], row_got.at[shard], row_sem).start()

        def send_rows(step, carry):
            there = (shard + step) % 32
            pltpu.make_async_remote_copy(
                row_send.at[there], row_got.at[shard], row_sent, row_sem, device_id=(section, there), device_id_type=MESH
            ).start()
            return carry

        lax.fori_loop(1, 32, send_rows, 0)
        pltpu.make_async_copy(row_got, row_got, row_sem).wait()
        where, block = position(lax.broadcasted_iota(jnp.int32, (LIVE, 512), 1))
        at = lax.broadcasted_iota(jnp.int32, (LIVE, 512), 0)
        rows = row_got[...].reshape(512, BLOCK)
        for b in range(2):
            pick = jnp.where((where == at) & (block == b), 1.0, 0.0).astype(jnp.bfloat16)
            compact = jnp.dot(pick, rows, preferred_element_type=jnp.float32).astype(jnp.bfloat16)
            first[:, b] = compact.reshape(UNITS, ROWS, BLOCK)

        def send_first(unit, carry):
            pltpu.make_async_copy(first.at[unit], gathered.at[unit, pl.ds(own, 2)], gather_sem.at[unit]).start()
            for step in SEND_ORDER[:-1]:
                pltpu.make_async_remote_copy(
                    first.at[unit],
                    gathered.at[unit, pl.ds(own, 2)],
                    first_sent.at[unit],
                    gather_sem.at[unit],
                    device_id=(section, chip_at(step) * 2 + core),
                    device_id_type=MESH,
                ).start()
            return carry

        pltpu.make_async_copy(row_got.at[pl.ds(0, 31)], row_got.at[pl.ds(0, 31)], row_sent).wait()
        lax.fori_loop(0, UNITS, send_first, 0)

    for load in loads:
        load.wait()
    zero_tile = jnp.zeros((BLOCK, BLOCK), jnp.bfloat16)
    for j in range(HB):
        down_tiles[j, KMAX] = zero_tile
    normed[NB] = jnp.zeros((ROWS, BLOCK), jnp.bfloat16)

    def widen(block, carry):
        columns = pl.ds(pl.multiple_of(block * BLOCK, BLOCK), BLOCK)
        for side, start in ((0, other_half), (1, half)):
            for j in range(HB):
                down_dense[side, pl.ds(j * BLOCK, BLOCK), columns] = down_tiles[j, inverse[j, start + block]]
        return carry

    lax.fori_loop(0, HALF, widen, 0)

    def work(unit):
        mine = gathered.at[unit, pl.ds(half, HALF)]
        theirs = gathered.at[unit, pl.ds(other_half, HALF)]
        pltpu.make_async_copy(mine, mine, gather_sem.at[unit]).wait()
        pltpu.make_async_remote_copy(
            mine, mine, core_sent.at[unit], core_sem.at[unit], device_id=partner, device_id_type=MESH
        ).start()

        squares = jnp.zeros((ROWS, BLOCK), jnp.float32)

        def scale(start, squares):
            for b in range(HALF):
                x = gathered[unit, start + b].astype(jnp.float32)
                squares = squares + x * x
                columns = pl.ds(pl.multiple_of((start + b) * BLOCK, BLOCK), BLOCK)
                normed[start + b] = (x * gain[0:1, columns]).astype(jnp.bfloat16)
            return squares

        squares = scale(half, squares)
        pltpu.make_async_copy(theirs, theirs, core_sem.at[unit]).wait()
        squares = scale(other_half, squares)
        mean = jnp.sum(squares, axis=-1, keepdims=True) * (1.0 / (NB * BLOCK))
        row_scale = lax.rsqrt(mean + NORM_EPS)

        hidden = []
        for j in range(HB):
            picked = []
            for k in range(KMAX):
                slot = in_index[j, k]
                picked.append(normed[jnp.where(slot < 0, NB, slot)])
            both = jnp.dot(
                jnp.concatenate(picked, axis=1), gate_up[j], preferred_element_type=jnp.float32
            )
            gate_val = both[:, :BLOCK] * row_scale
            up_val = both[:, BLOCK:] * row_scale
            hidden.append((gate_val / (1.0 + jnp.exp(-gate_val)) * up_val).astype(jnp.bfloat16))
        hidden = jnp.concatenate(hidden, axis=1)

        partial = jnp.dot(hidden, down_dense[0], preferred_element_type=jnp.float32)
        for b in range(HALF):
            given[unit, b] = partial[:, b * BLOCK : (b + 1) * BLOCK].astype(jnp.bfloat16)
        pltpu.make_async_remote_copy(
            given.at[unit], core_got.at[unit], pair_sent.at[unit], pair_sem.at[unit], device_id=partner, device_id_type=MESH
        ).start()
        partial = jnp.dot(hidden, down_dense[1], preferred_element_type=jnp.float32)
        for b in range(HALF):
            kept[b] = partial[:, b * BLOCK : (b + 1) * BLOCK]
        pltpu.make_async_copy(core_got.at[unit], core_got.at[unit], pair_sem.at[unit]).wait()
        for b in range(HALF):
            summed[unit, b] = (kept[b] + core_got[unit, b].astype(jnp.float32)).astype(jnp.bfloat16)
        for step in SEND_ORDER[:-1]:
            there = chip_at(step)
            pltpu.make_async_remote_copy(
                summed.at[unit, pl.ds(there * 2, 2)],
                got.at[unit, chip],
                scatter_sent.at[unit],
                scatter_sem.at[unit],
                device_id=(section, there * 2 + core),
                device_id_type=MESH,
            ).start()
        pltpu.make_async_copy(
            summed.at[unit, pl.ds(chip * 2, 2)], got.at[unit, chip], scatter_sem.at[unit]
        ).start()

    def finish(unit):
        pltpu.make_async_copy(got.at[unit], got.at[unit], scatter_sem.at[unit]).wait()
        for b in range(2):
            total = got[unit, 0, b].astype(jnp.float32)
            for c in range(1, CHIPS):
                total = total + got[unit, c, b].astype(jnp.float32)
            result[unit, b] = (gathered[unit, own + b].astype(jnp.float32) + total).astype(jnp.bfloat16)

        @pl.when(section < SECTIONS - 1)
        def _():
            for step in SEND_ORDER:
                pltpu.make_async_remote_copy(
                    result.at[unit],
                    gathered.at[unit, pl.ds(own, 2)],
                    gather_sent.at[unit],
                    gather_sem.at[unit],
                    device_id=(section + 1, chip_at(step) * 2 + core),
                    device_id_type=MESH,
                ).start()

    def turn(unit, carry):
        @pl.when(unit < UNITS)
        def _():
            work(unit)

        @pl.when(unit > 0)
        def _():
            finish(unit - 1)

        return carry

    lax.fori_loop(0, UNITS + 1, turn, 0)

    where, block = position(lax.broadcasted_iota(jnp.int32, (512, LIVE), 0))
    at = lax.broadcasted_iota(jnp.int32, (512, LIVE), 1)
    spread = jnp.zeros((512, BLOCK), jnp.float32)
    for b in range(2):
        place = jnp.where((where == at) & (block == b), 1.0, 0.0).astype(jnp.bfloat16)
        spread = spread + jnp.dot(place, result[:, b].reshape(LIVE, BLOCK), preferred_element_type=jnp.float32)
    out_send[...] = spread.astype(jnp.bfloat16).reshape(32, 16, BLOCK)
    pltpu.make_async_copy(out_send.at[shard], out_got.at[shard], out_sem).start()

    def send_out(step, carry):
        there = (shard + step) % 32
        pltpu.make_async_remote_copy(
            out_send.at[there], out_got.at[shard], out_sent, out_sem, device_id=(section, there), device_id_type=MESH
        ).start()
        return carry

    lax.fori_loop(1, 32, send_out, 0)

    def drain(unit, carry):
        mine = gathered.at[unit, pl.ds(half, HALF)]
        sent = got.at[unit, pl.ds(0, CHIPS - 1)]
        pltpu.make_async_copy(mine, mine, core_sent.at[unit]).wait()
        pltpu.make_async_copy(given.at[unit], given.at[unit], pair_sent.at[unit]).wait()
        pltpu.make_async_copy(sent, sent, scatter_sent.at[unit]).wait()

        @pl.when(section < SECTIONS - 1)
        def _():
            pltpu.make_async_copy(got.at[unit], got.at[unit], gather_sent.at[unit]).wait()

        @pl.when(section == 0)
        def _():
            pltpu.make_async_copy(sent, sent, first_sent.at[unit]).wait()

        return carry

    lax.fori_loop(0, UNITS, drain, 0)
    pltpu.make_async_copy(out_got, out_got, out_sem).wait()
    for b in range(NB):
        owner = b % HALF // 2 * 2 + b // HALF
        out[:, pl.ds(b * BLOCK, BLOCK)] = out_got[owner, pl.ds(b % 2 * 8, 8), :]
    pltpu.make_async_copy(out_got.at[pl.ds(0, 31)], out_got.at[pl.ds(0, 31)], out_sent).wait()


def body(tokens, lengths, norm_gain, gate_tiles, up_tiles, in_index, down_tiles, out_index):
    slots = jnp.arange(KMAX, dtype=jnp.int32)
    hit = out_index[0][:, None, :] == jnp.arange(NB, dtype=jnp.int32)[None, :, None]
    inverse = jnp.min(jnp.where(hit, slots, KMAX), axis=-1)
    bf16 = functools.partial(pltpu.VMEM, dtype=jnp.bfloat16)
    dma = pltpu.SemaphoreType.DMA
    smem = pl.BlockSpec(memory_space=pltpu.SMEM)
    vmem = pl.BlockSpec(memory_space=pltpu.VMEM)
    hbm = pl.BlockSpec(memory_space=pl.ANY)
    rows = pl.pallas_call(
        kernel,
        out_shape=jax.ShapeDtypeStruct((8, NB * BLOCK), jnp.bfloat16),
        in_specs=[smem, smem, smem, vmem, vmem, hbm, hbm, hbm],
        out_specs=vmem,
        scratch_shapes=[
            bf16((HB, KMAX * BLOCK, 2 * BLOCK)),
            bf16((HB, KMAX + 1, BLOCK, BLOCK)),
            bf16((2, HB * BLOCK, HALF * BLOCK)),
            bf16((UNITS, NB, ROWS, BLOCK)),
            bf16((NB + 1, ROWS, BLOCK)),
            bf16((UNITS, HALF, ROWS, BLOCK)),
            pltpu.VMEM((HALF, ROWS, BLOCK), jnp.float32),
            bf16((UNITS, HALF, ROWS, BLOCK)),
            bf16((UNITS, HALF, ROWS, BLOCK)),
            bf16((UNITS, CHIPS, 2, ROWS, BLOCK)),
            bf16((UNITS, 2, ROWS, BLOCK)),
            bf16((UNITS, 2, ROWS, BLOCK)),
            bf16((32, 16, BLOCK)),
            bf16((32, 16, BLOCK)),
            bf16((32, 16, BLOCK)),
            bf16((32, 16, BLOCK)),
            dma((3, HB)),
            dma((UNITS,)),
            dma((UNITS,)),
            dma((UNITS,)),
            dma((UNITS,)),
            dma((UNITS,)),
            dma((UNITS,)),
            dma((UNITS,)),
            dma((UNITS,)),
            dma((UNITS,)),
            dma,
            dma,
            dma,
            dma,
        ],
        compiler_params=pltpu.CompilerParams(
            collective_id=0, has_side_effects=True, vmem_limit_bytes=52 * 1024 * 1024
        ),
        name="relay",
    )(
        lengths,
        in_index[0],
        inverse,
        tokens.reshape(8, NB * BLOCK),
        norm_gain,
        gate_tiles.reshape(HB, KMAX * BLOCK, BLOCK),
        up_tiles.reshape(HB, KMAX * BLOCK, BLOCK),
        down_tiles.reshape(HB, KMAX, BLOCK, BLOCK),
    )
    return rows.reshape(1, 4, 2, NB * BLOCK)


def solution(mesh):
    placed = (
        P(None, "shard", None),
        P(),
        P("section", None),
        P("section", "shard", None, None, None),
        P("section", "shard", None, None, None),
        P("section", "shard", None),
        P("section", "shard", None, None, None),
        P("section", "shard", None),
    )
    return jax.shard_map(
        body,
        mesh=mesh,
        in_specs=placed,
        out_specs=P("section", None, "shard", None),
        check_vma=False,
    )
```

```python
import functools

import jax
import jax.numpy as jnp
from jax import lax
from jax.experimental import pallas as pl
from jax.experimental.pallas import tpu as pltpu
from jax.sharding import PartitionSpec as P

NORM_EPS = 1e-05
LIVE = 160
ROWS = 16
UNITS = LIVE // ROWS
SIDE = 4
CHIPS = SIDE * SIDE
SECTIONS = 8
BLOCK = 128
NB = 64
HALF = NB // 2
HB = 4
KMAX = 28
LAG = 3
LEAD = 4
MESH = pl.DeviceIdType.MESH
SEND_ORDER = sorted(range(CHIPS), key=lambda step: -sum(min(d, SIDE - d) for d in divmod(step, SIDE)))


def kernel(
    lengths_in, in_index_in, out_index_in, tokens_in, gain_in, gate, up, down, out,
    lengths, in_index, out_index, inverse, inverse_rows, tokens, gain,
    gate_up, down_tiles, parts, gathered, normed, given, kept, core_got, summed, got, first, result,
    row_send, row_got, out_send, out_got,
    small_sem, load_sem, gather_sem, gather_sent, core_sem, core_sent, pair_sem, pair_sent,
    scatter_sem, scatter_sent, first_sent, row_sem, row_sent, out_sem, out_sent,
):
    section = lax.axis_index("section")
    shard = lax.axis_index("shard")
    chip = shard // 2
    core = shard % 2
    chip_y = chip // SIDE
    chip_x = chip % SIDE
    half = core * HALF
    other_half = HALF - half
    own = half + chip * 2
    partner = (section, chip * 2 + 1 - core)

    smalls = [
        pltpu.make_async_copy(lengths_in, lengths, small_sem.at[0]),
        pltpu.make_async_copy(in_index_in, in_index, small_sem.at[1]),
        pltpu.make_async_copy(out_index_in, out_index, small_sem.at[2]),
        pltpu.make_async_copy(tokens_in, tokens, small_sem.at[3]),
        pltpu.make_async_copy(gain_in, gain, small_sem.at[4]),
    ]
    for small in smalls:
        small.start()
    loads = []
    for j in range(HB):
        loads.append(pltpu.make_async_copy(gate.at[j], gate_up.at[j, :, pl.ds(0, BLOCK)], load_sem.at[0, j]))
        loads.append(pltpu.make_async_copy(up.at[j], gate_up.at[j, :, pl.ds(BLOCK, BLOCK)], load_sem.at[1, j]))
        loads.append(pltpu.make_async_copy(down.at[j], down_tiles.at[j], load_sem.at[2, j]))
    for load in loads:
        load.start()

    def chip_at(step):
        return (chip_y + step // SIDE) % SIDE * SIDE + (chip_x + step % SIDE) % SIDE

    barrier = pltpu.get_barrier_semaphore()
    before = (section + SECTIONS - 1) % SECTIONS

    def greet_plane(step, carry):
        pl.semaphore_signal(barrier, inc=1, device_id=(section, (shard + step) % 32), device_id_type=MESH)
        return carry

    def greet_before(step, carry):
        pl.semaphore_signal(barrier, inc=1, device_id=(before, step * 2 + core), device_id_type=MESH)
        return carry

    lax.fori_loop(1, 32, greet_plane, 0)
    lax.fori_loop(0, CHIPS, greet_before, 0)

    for small in smalls:
        small.wait()
    offsets = [jnp.int32(0)]
    for m in range(3):
        offsets.append(offsets[-1] + lengths[m])

    def position(index):
        block = (index >> 3) & 1
        micro = (index >> 1) & 3
        row = (index >> 4) * 2 + (index & 1)
        start = jnp.full_like(index, 0)
        length = jnp.full_like(index, lengths[0])
        for m in range(1, 4):
            start = jnp.where(micro == m, offsets[m], start)
            length = jnp.where(micro == m, lengths[m], length)
        return jnp.where(row < length, start + row, -1), block

    blocks = lax.broadcasted_iota(jnp.int32, (1, BLOCK), 1)
    for j in range(HB):
        row = jnp.full((1, BLOCK), KMAX, jnp.int32)
        for k in range(KMAX):
            row = jnp.where(blocks == out_index[0, j, k], k, row)
        inverse_rows[j : j + 1, :] = row
    inverse_copy = pltpu.make_async_copy(inverse_rows, inverse, small_sem.at[5])
    inverse_copy.start()
    for j in range(HB):
        parts[j, KMAX] = jnp.zeros((ROWS, BLOCK), jnp.float32)
    normed[NB] = jnp.zeros((ROWS, BLOCK), jnp.bfloat16)

    @pl.when(section == 0)
    def _():
        for b in range(NB):
            owner = b % HALF // 2 * 2 + b // HALF
            rows = [tokens[m, :, pl.ds(b * BLOCK, BLOCK)].astype(jnp.float32) for m in range(4)]
            row_send[owner, pl.ds(b % 2 * 8, 8), :] = jnp.concatenate(rows, axis=0).astype(jnp.bfloat16)

    inverse_copy.wait()
    pl.semaphore_wait(barrier, 31 + CHIPS)

    @pl.when(section == 0)
    def _():
        pltpu.make_async_copy(row_send.at[shard], row_got.at[shard], row_sem).start()

        def send_rows(step, carry):
            there = (shard + step) % 32
            pltpu.make_async_remote_copy(
                row_send.at[there], row_got.at[shard], row_sent, row_sem, device_id=(section, there), device_id_type=MESH
            ).start()
            return carry

        lax.fori_loop(1, 32, send_rows, 0)

    for load in loads:
        load.wait()

    def send_first(unit):
        pltpu.make_async_copy(first.at[unit], gathered.at[unit, pl.ds(own, 2)], gather_sem.at[unit]).start()
        for step in SEND_ORDER[:-1]:
            pltpu.make_async_remote_copy(
                first.at[unit],
                gathered.at[unit, pl.ds(own, 2)],
                first_sent.at[unit],
                gather_sem.at[unit],
                device_id=(section, chip_at(step) * 2 + core),
                device_id_type=MESH,
            ).start()

    @pl.when(section == 0)
    def _():
        where, block = position(lax.broadcasted_iota(jnp.int32, (LIVE, 512), 1))
        at = lax.broadcasted_iota(jnp.int32, (LIVE, 512), 0)
        picks = [jnp.where((where == at) & (block == b), 1.0, 0.0).astype(jnp.bfloat16) for b in range(2)]
        pltpu.make_async_copy(row_got, row_got, row_sem).wait()
        rows = row_got[...].reshape(512, BLOCK)
        for b in range(2):
            compact = jnp.dot(picks[b], rows, preferred_element_type=jnp.float32).astype(jnp.bfloat16)
            first[:, b] = compact.reshape(UNITS, ROWS, BLOCK)
        for unit in range(LEAD):
            send_first(unit)
        pltpu.make_async_copy(row_got.at[pl.ds(0, 31)], row_got.at[pl.ds(0, 31)], row_sent).wait()

    def scale(unit, start):
        total = jnp.zeros((ROWS, BLOCK), jnp.float32)
        for b in range(HALF):
            x = gathered[unit, start + b].astype(jnp.float32)
            total = total + x * x
            columns = pl.ds(pl.multiple_of((start + b) * BLOCK, BLOCK), BLOCK)
            normed[start + b] = (x * gain[0:1, columns]).astype(jnp.bfloat16)
        return total

    def arrive(unit):
        mine = gathered.at[unit, pl.ds(half, HALF)]
        pltpu.make_async_copy(mine, mine, gather_sem.at[unit]).wait()
        pltpu.make_async_remote_copy(
            mine, mine, core_sent.at[unit], core_sem.at[unit], device_id=partner, device_id_type=MESH
        ).start()

    def multiply(unit):
        total = scale(unit, half)
        theirs = gathered.at[unit, pl.ds(other_half, HALF)]
        pltpu.make_async_copy(theirs, theirs, core_sem.at[unit]).wait()
        total = total + scale(unit, other_half)
        mean = jnp.sum(total, axis=-1, keepdims=True) * (1.0 / (NB * BLOCK))
        row_scale = lax.rsqrt(mean + NORM_EPS)

        both = []
        for j in range(HB):
            picked = []
            for k in range(KMAX):
                slot = in_index[0, j, k]
                picked.append(normed[jnp.where(slot < 0, NB, slot)])
            both.append(
                jnp.dot(jnp.concatenate(picked, axis=1), gate_up[j], preferred_element_type=jnp.float32)
            )
        hidden = []
        for j in range(HB):
            gate_val = both[j][:, :BLOCK] * row_scale
            up_val = both[j][:, BLOCK:] * row_scale
            hidden.append((gate_val / (1.0 + jnp.exp(-gate_val)) * up_val).astype(jnp.bfloat16))

        for k in range(0, KMAX, 2):
            for j in range(HB):
                two = jnp.concatenate([down_tiles[j, k], down_tiles[j, k + 1]], axis=1)
                product = jnp.dot(hidden[j], two, preferred_element_type=jnp.float32)
                parts[j, k] = product[:, :BLOCK]
                parts[j, k + 1] = product[:, BLOCK:]

        def total_of(block):
            total = parts[0, inverse[0, block]]
            for j in range(1, HB):
                total = total + parts[j, inverse[j, block]]
            return total

        for b in range(HALF):
            given[unit, b] = total_of(other_half + b).astype(jnp.bfloat16)
        pltpu.make_async_remote_copy(
            given.at[unit], core_got.at[unit], pair_sent.at[unit], pair_sem.at[unit], device_id=partner, device_id_type=MESH
        ).start()
        for b in range(HALF):
            kept[b] = total_of(half + b)

    def scatter(unit):
        pltpu.make_async_copy(core_got.at[unit], core_got.at[unit], pair_sem.at[unit]).wait()
        for b in range(HALF):
            summed[unit, b] = (kept[b] + core_got[unit, b].astype(jnp.float32)).astype(jnp.bfloat16)
        for step in SEND_ORDER[:-1]:
            there = chip_at(step)
            pltpu.make_async_remote_copy(
                summed.at[unit, pl.ds(there * 2, 2)],
                got.at[unit, chip],
                scatter_sent.at[unit],
                scatter_sem.at[unit],
                device_id=(section, there * 2 + core),
                device_id_type=MESH,
            ).start()
        pltpu.make_async_copy(
            summed.at[unit, pl.ds(chip * 2, 2)], got.at[unit, chip], scatter_sem.at[unit]
        ).start()

    def finish(unit):
        pltpu.make_async_copy(got.at[unit], got.at[unit], scatter_sem.at[unit]).wait()
        for b in range(2):
            total = got[unit, 0, b].astype(jnp.float32)
            for c in range(1, CHIPS):
                total = total + got[unit, c, b].astype(jnp.float32)
            result[unit, b] = (gathered[unit, own + b].astype(jnp.float32) + total).astype(jnp.bfloat16)

        @pl.when(section < SECTIONS - 1)
        def _():
            for step in SEND_ORDER:
                pltpu.make_async_remote_copy(
                    result.at[unit],
                    gathered.at[unit, pl.ds(own, 2)],
                    gather_sent.at[unit],
                    gather_sem.at[unit],
                    device_id=(section + 1, chip_at(step) * 2 + core),
                    device_id_type=MESH,
                ).start()

    def turn(now, carry):
        @pl.when(now < UNITS)
        def _():
            arrive(now)

        @pl.when(now >= LAG)
        def _():
            finish(now - LAG)

        @pl.when((section == 0) & (now + LEAD < UNITS))
        def _():
            send_first(now + LEAD)

        @pl.when((now >= 1) & (now <= UNITS))
        def _():
            scatter(now - 1)

        @pl.when(now < UNITS)
        def _():
            multiply(now)

        return carry

    lax.fori_loop(0, UNITS + LAG, turn, 0)

    where, block = position(lax.broadcasted_iota(jnp.int32, (512, LIVE), 0))
    at = lax.broadcasted_iota(jnp.int32, (512, LIVE), 1)
    spread = jnp.zeros((512, BLOCK), jnp.float32)
    for b in range(2):
        place = jnp.where((where == at) & (block == b), 1.0, 0.0).astype(jnp.bfloat16)
        spread = spread + jnp.dot(place, result[:, b].reshape(LIVE, BLOCK), preferred_element_type=jnp.float32)
    out_send[...] = spread.astype(jnp.bfloat16).reshape(32, 16, BLOCK)
    pltpu.make_async_copy(out_send.at[shard], out_got.at[shard], out_sem).start()

    def send_out(step, carry):
        there = (shard + step) % 32
        pltpu.make_async_remote_copy(
            out_send.at[there], out_got.at[shard], out_sent, out_sem, device_id=(section, there), device_id_type=MESH
        ).start()
        return carry

    lax.fori_loop(1, 32, send_out, 0)

    def drain(unit, carry):
        mine = gathered.at[unit, pl.ds(half, HALF)]
        sent = got.at[unit, pl.ds(0, CHIPS - 1)]
        pltpu.make_async_copy(mine, mine, core_sent.at[unit]).wait()
        pltpu.make_async_copy(given.at[unit], given.at[unit], pair_sent.at[unit]).wait()
        pltpu.make_async_copy(sent, sent, scatter_sent.at[unit]).wait()

        @pl.when(section < SECTIONS - 1)
        def _():
            pltpu.make_async_copy(got.at[unit], got.at[unit], gather_sent.at[unit]).wait()

        @pl.when(section == 0)
        def _():
            pltpu.make_async_copy(sent, sent, first_sent.at[unit]).wait()

        return carry

    lax.fori_loop(0, UNITS, drain, 0)
    pltpu.make_async_copy(out_got, out_got, out_sem).wait()
    for b in range(NB):
        owner = b % HALF // 2 * 2 + b // HALF
        out[:, pl.ds(b * BLOCK, BLOCK)] = out_got[owner, pl.ds(b % 2 * 8, 8), :]
    pltpu.make_async_copy(out_got.at[pl.ds(0, 31)], out_got.at[pl.ds(0, 31)], out_sent).wait()


def body(tokens, lengths, norm_gain, gate_tiles, up_tiles, in_index, down_tiles, out_index):
    bf16 = functools.partial(pltpu.VMEM, dtype=jnp.bfloat16)
    dma = pltpu.SemaphoreType.DMA
    vmem = pl.BlockSpec(memory_space=pltpu.VMEM)
    hbm = pl.BlockSpec(memory_space=pltpu.HBM)
    rows = pl.pallas_call(
        kernel,
        out_shape=jax.ShapeDtypeStruct((8, NB * BLOCK), jnp.bfloat16),
        in_specs=[hbm] * 8,
        out_specs=vmem,
        scratch_shapes=[
            pltpu.SMEM((4,), jnp.int32),
            pltpu.SMEM((1, HB, KMAX), jnp.int32),
            pltpu.SMEM((1, HB, KMAX), jnp.int32),
            pltpu.SMEM((HB, BLOCK), jnp.int32),
            pltpu.VMEM((HB, BLOCK), jnp.int32),
            bf16((4, 2, NB * BLOCK)),
            pltpu.VMEM((1, NB * BLOCK), jnp.float32),
            bf16((HB, KMAX * BLOCK, 2 * BLOCK)),
            bf16((HB, KMAX, BLOCK, BLOCK)),
            pltpu.VMEM((HB, KMAX + 1, ROWS, BLOCK), jnp.float32),
            bf16((UNITS, NB, ROWS, BLOCK)),
            bf16((NB + 1, ROWS, BLOCK)),
            bf16((UNITS, HALF, ROWS, BLOCK)),
            pltpu.VMEM((HALF, ROWS, BLOCK), jnp.float32),
            bf16((UNITS, HALF, ROWS, BLOCK)),
            bf16((UNITS, HALF, ROWS, BLOCK)),
            bf16((UNITS, CHIPS, 2, ROWS, BLOCK)),
            bf16((UNITS, 2, ROWS, BLOCK)),
            bf16((UNITS, 2, ROWS, BLOCK)),
            bf16((32, 16, BLOCK)),
            bf16((32, 16, BLOCK)),
            bf16((32, 16, BLOCK)),
            bf16((32, 16, BLOCK)),
            dma((6,)),
            dma((3, HB)),
            dma((UNITS,)),
            dma((UNITS,)),
            dma((UNITS,)),
            dma((UNITS,)),
            dma((UNITS,)),
            dma((UNITS,)),
            dma((UNITS,)),
            dma((UNITS,)),
            dma((UNITS,)),
            dma,
            dma,
            dma,
            dma,
        ],
        compiler_params=pltpu.CompilerParams(
            collective_id=0, has_side_effects=True, vmem_limit_bytes=60 * 1024 * 1024
        ),
        name="relay",
    )(
        lengths,
        in_index,
        out_index,
        tokens,
        norm_gain,
        gate_tiles.reshape(HB, KMAX * BLOCK, BLOCK),
        up_tiles.reshape(HB, KMAX * BLOCK, BLOCK),
        down_tiles.reshape(HB, KMAX, BLOCK, BLOCK),
    )
    return rows.reshape(1, 4, 2, NB * BLOCK)


def solution(mesh):
    placed = (
        P(None, "shard", None),
        P(),
        P("section", None),
        P("section", "shard", None, None, None),
        P("section", "shard", None, None, None),
        P("section", "shard", None),
        P("section", "shard", None, None, None),
        P("section", "shard", None),
    )
    return jax.shard_map(
        body,
        mesh=mesh,
        in_specs=placed,
        out_specs=P("section", None, "shard", None),
        check_vma=False,
    )
```

```python
import functools

import jax
import jax.numpy as jnp
from jax import lax
from jax.experimental import pallas as pl
from jax.experimental.pallas import tpu as pltpu
from jax.sharding import PartitionSpec as P

NORM_EPS = 1e-05
LIVE = 160
ROWS = 16
UNITS = LIVE // ROWS
SIDE = 4
CHIPS = SIDE * SIDE
SECTIONS = 8
BLOCK = 128
NB = 64
HALF = NB // 2
HB = 4
PIECE = 16
KMAX = 28
LAG = 3
LEAD = 4
MESH = pl.DeviceIdType.MESH
SEND_ORDER = sorted(range(CHIPS), key=lambda step: -sum(min(d, SIDE - d) for d in divmod(step, SIDE)))


def kernel(
    lengths_in, in_index_in, out_index_in, tokens_in, gain_in, gate, up, down, out,
    lengths, in_index, out_index, inverse, inverse_rows, tokens, gain,
    gate_up, down_tiles, parts, gathered, normed, given, kept, core_got, summed, got, first, result,
    row_send, row_got, out_send, out_got,
    small_sem, load_sem, gather_sem, gather_sent, core_sem, core_sent, pair_sem, pair_sent,
    scatter_sem, scatter_sent, first_sent, row_sem, row_sent, out_sem, out_sent,
):
    section = lax.axis_index("section")
    shard = lax.axis_index("shard")
    chip = shard // 2
    core = shard % 2
    chip_y = chip // SIDE
    chip_x = chip % SIDE
    half = core * HALF
    other_half = HALF - half
    own = half + chip * 2
    partner = (section, chip * 2 + 1 - core)

    smalls = [
        pltpu.make_async_copy(lengths_in, lengths, small_sem.at[0]),
        pltpu.make_async_copy(in_index_in, in_index, small_sem.at[1]),
        pltpu.make_async_copy(out_index_in, out_index, small_sem.at[2]),
        pltpu.make_async_copy(tokens_in, tokens, small_sem.at[3]),
        pltpu.make_async_copy(gain_in, gain, small_sem.at[4]),
    ]
    for small in smalls:
        small.start()
    loads = []
    for j in range(HB):
        loads.append(pltpu.make_async_copy(gate.at[j], gate_up.at[j, :, pl.ds(0, BLOCK)], load_sem.at[0, j]))
        loads.append(pltpu.make_async_copy(up.at[j], gate_up.at[j, :, pl.ds(BLOCK, BLOCK)], load_sem.at[1, j]))
        loads.append(pltpu.make_async_copy(down.at[j], down_tiles.at[j], load_sem.at[2, j]))
    for load in loads:
        load.start()

    ys = [(chip_y + step) % SIDE * SIDE for step in range(SIDE)]
    xs = [(chip_x + step) % SIDE for step in range(SIDE)]
    chips = [y + x for y in ys for x in xs]
    peers = [there * 2 + core for there in chips]

    barrier = pltpu.get_barrier_semaphore()
    before = (section + SECTIONS - 1) % SECTIONS

    def greet_plane(step, carry):
        pl.semaphore_signal(barrier, inc=1, device_id=(section, (shard + step) % 32), device_id_type=MESH)
        return carry

    def greet_before(step, carry):
        pl.semaphore_signal(barrier, inc=1, device_id=(before, step * 2 + core), device_id_type=MESH)
        return carry

    lax.fori_loop(1, 32, greet_plane, 0)
    lax.fori_loop(0, CHIPS, greet_before, 0)

    for small in smalls:
        small.wait()
    offsets = [jnp.int32(0)]
    for m in range(3):
        offsets.append(offsets[-1] + lengths[m])

    def position(index):
        block = (index >> 3) & 1
        micro = (index >> 1) & 3
        row = (index >> 4) * 2 + (index & 1)
        start = jnp.full_like(index, 0)
        length = jnp.full_like(index, lengths[0])
        for m in range(1, 4):
            start = jnp.where(micro == m, offsets[m], start)
            length = jnp.where(micro == m, lengths[m], length)
        return jnp.where(row < length, start + row, -1), block

    blocks = lax.broadcasted_iota(jnp.int32, (1, BLOCK), 1)
    for j in range(HB):
        row = jnp.full((1, BLOCK), KMAX, jnp.int32)
        for k in range(KMAX):
            row = jnp.where(blocks == out_index[0, j, k], k, row)
        inverse_rows[j : j + 1, :] = row
    inverse_copy = pltpu.make_async_copy(inverse_rows, inverse, small_sem.at[5])
    inverse_copy.start()
    for j in range(HB):
        parts[j, KMAX] = jnp.zeros((ROWS, BLOCK), jnp.float32)
    normed[NB] = jnp.zeros((ROWS, BLOCK), jnp.bfloat16)

    @pl.when(section == 0)
    def _():
        for b in range(NB):
            owner = b % HALF // 2 * 2 + b // HALF
            rows = [tokens[m, :, pl.ds(b * BLOCK, BLOCK)].astype(jnp.float32) for m in range(4)]
            row_send[owner, pl.ds(b % 2 * 8, 8), :] = jnp.concatenate(rows, axis=0).astype(jnp.bfloat16)

    inverse_copy.wait()
    pl.semaphore_wait(barrier, 31 + CHIPS)

    @pl.when(section == 0)
    def _():
        pltpu.make_async_copy(row_send.at[shard], row_got.at[shard], row_sem).start()

        def send_rows(step, carry):
            there = (shard + step) % 32
            pltpu.make_async_remote_copy(
                row_send.at[there], row_got.at[shard], row_sent, row_sem, device_id=(section, there), device_id_type=MESH
            ).start()
            return carry

        lax.fori_loop(1, 32, send_rows, 0)

    for load in loads:
        load.wait()

    def send_first(unit):
        pltpu.make_async_copy(first.at[unit], gathered.at[unit, pl.ds(own, 2)], gather_sem.at[unit, chip // 8]).start()
        for step in SEND_ORDER[:-1]:
            pltpu.make_async_remote_copy(
                first.at[unit],
                gathered.at[unit, pl.ds(own, 2)],
                first_sent.at[unit],
                gather_sem.at[unit, chip // 8],
                device_id=(section, peers[step]),
                device_id_type=MESH,
            ).start()

    @pl.when(section == 0)
    def _():
        where, block = position(lax.broadcasted_iota(jnp.int32, (LIVE, 512), 1))
        at = lax.broadcasted_iota(jnp.int32, (LIVE, 512), 0)
        picks = [jnp.where((where == at) & (block == b), 1.0, 0.0).astype(jnp.bfloat16) for b in range(2)]
        pltpu.make_async_copy(row_got, row_got, row_sem).wait()
        rows = row_got[...].reshape(512, BLOCK)
        for b in range(2):
            compact = jnp.dot(picks[b], rows, preferred_element_type=jnp.float32).astype(jnp.bfloat16)
            first[:, b] = compact.reshape(UNITS, ROWS, BLOCK)
        for unit in range(LEAD):
            send_first(unit)
        pltpu.make_async_copy(row_got.at[pl.ds(0, 31)], row_got.at[pl.ds(0, 31)], row_sent).wait()

    def scale(unit, start):
        total = jnp.zeros((ROWS, BLOCK), jnp.float32)
        for b in range(PIECE):
            x = gathered[unit, start + b].astype(jnp.float32)
            total = total + x * x
            columns = pl.ds(pl.multiple_of((start + b) * BLOCK, BLOCK), BLOCK)
            normed[start + b] = (x * gain[0:1, columns]).astype(jnp.bfloat16)
        return total

    def arrive(unit):
        for piece in range(2):
            mine = gathered.at[unit, pl.ds(half + piece * PIECE, PIECE)]
            pltpu.make_async_copy(mine, mine, gather_sem.at[unit, piece]).wait()
            pltpu.make_async_remote_copy(
                mine, mine, core_sent.at[unit, piece], core_sem.at[unit, piece], device_id=partner, device_id_type=MESH
            ).start()

    def multiply(unit):
        total = scale(unit, half) + scale(unit, half + PIECE)
        for piece in range(2):
            theirs = gathered.at[unit, pl.ds(other_half + piece * PIECE, PIECE)]
            pltpu.make_async_copy(theirs, theirs, core_sem.at[unit, piece]).wait()
            total = total + scale(unit, other_half + piece * PIECE)
        mean = jnp.sum(total, axis=-1, keepdims=True) * (1.0 / (NB * BLOCK))
        row_scale = lax.rsqrt(mean + NORM_EPS)

        both = []
        for j in range(HB):
            picked = []
            for k in range(KMAX):
                slot = in_index[0, j, k]
                picked.append(normed[jnp.where(slot < 0, NB, slot)])
            both.append(
                jnp.dot(jnp.concatenate(picked, axis=1), gate_up[j], preferred_element_type=jnp.float32)
            )
        hidden = []
        for j in range(HB):
            gate_val = both[j][:, :BLOCK] * row_scale
            up_val = both[j][:, BLOCK:] * row_scale
            hidden.append((gate_val / (1.0 + jnp.exp(-gate_val)) * up_val).astype(jnp.bfloat16))

        for k in range(0, KMAX, 2):
            for j in range(HB):
                two = jnp.concatenate([down_tiles[j, k], down_tiles[j, k + 1]], axis=1)
                product = jnp.dot(hidden[j], two, preferred_element_type=jnp.float32)
                parts[j, k] = product[:, :BLOCK]
                parts[j, k + 1] = product[:, BLOCK:]

        def total_of(block):
            total = parts[0, inverse[0, block]]
            for j in range(1, HB):
                total = total + parts[j, inverse[j, block]]
            return total

        for b in range(HALF):
            given[unit, b] = total_of(other_half + b).astype(jnp.bfloat16)
        pltpu.make_async_remote_copy(
            given.at[unit], core_got.at[unit], pair_sent.at[unit], pair_sem.at[unit], device_id=partner, device_id_type=MESH
        ).start()
        for b in range(HALF):
            kept[b] = total_of(half + b)

    def scatter(unit):
        pltpu.make_async_copy(core_got.at[unit], core_got.at[unit], pair_sem.at[unit]).wait()
        for b in range(HALF):
            summed[unit, b] = (kept[b] + core_got[unit, b].astype(jnp.float32)).astype(jnp.bfloat16)
        for step in SEND_ORDER[:-1]:
            there = chips[step]
            pltpu.make_async_remote_copy(
                summed.at[unit, pl.ds(there * 2, 2)],
                got.at[unit, chip],
                scatter_sent.at[unit],
                scatter_sem.at[unit],
                device_id=(section, peers[step]),
                device_id_type=MESH,
            ).start()
        pltpu.make_async_copy(
            summed.at[unit, pl.ds(chip * 2, 2)], got.at[unit, chip], scatter_sem.at[unit]
        ).start()

    def finish(unit):
        pltpu.make_async_copy(got.at[unit], got.at[unit], scatter_sem.at[unit]).wait()
        for b in range(2):
            total = got[unit, 0, b].astype(jnp.float32)
            for c in range(1, CHIPS):
                total = total + got[unit, c, b].astype(jnp.float32)
            result[unit, b] = (gathered[unit, own + b].astype(jnp.float32) + total).astype(jnp.bfloat16)

        @pl.when(section < SECTIONS - 1)
        def _():
            for step in SEND_ORDER:
                pltpu.make_async_remote_copy(
                    result.at[unit],
                    gathered.at[unit, pl.ds(own, 2)],
                    gather_sent.at[unit],
                    gather_sem.at[unit, chip // 8],
                    device_id=(section + 1, peers[step]),
                    device_id_type=MESH,
                ).start()

    def turn(now, carry):
        @pl.when(now < UNITS)
        def _():
            arrive(now)

        @pl.when(now >= LAG)
        def _():
            finish(now - LAG)

        @pl.when((section == 0) & (now + LEAD < UNITS))
        def _():
            send_first(now + LEAD)

        @pl.when((now >= 1) & (now <= UNITS))
        def _():
            scatter(now - 1)

        @pl.when(now < UNITS)
        def _():
            multiply(now)

        return carry

    lax.fori_loop(0, UNITS + LAG, turn, 0)

    where, block = position(lax.broadcasted_iota(jnp.int32, (512, LIVE), 0))
    at = lax.broadcasted_iota(jnp.int32, (512, LIVE), 1)
    spread = jnp.zeros((512, BLOCK), jnp.float32)
    for b in range(2):
        place = jnp.where((where == at) & (block == b), 1.0, 0.0).astype(jnp.bfloat16)
        spread = spread + jnp.dot(place, result[:, b].reshape(LIVE, BLOCK), preferred_element_type=jnp.float32)
    out_send[...] = spread.astype(jnp.bfloat16).reshape(32, 16, BLOCK)
    pltpu.make_async_copy(out_send.at[shard], out_got.at[shard], out_sem).start()

    def send_out(step, carry):
        there = (shard + step) % 32
        pltpu.make_async_remote_copy(
            out_send.at[there], out_got.at[shard], out_sent, out_sem, device_id=(section, there), device_id_type=MESH
        ).start()
        return carry

    lax.fori_loop(1, 32, send_out, 0)

    def drain(unit, carry):
        sent = got.at[unit, pl.ds(0, CHIPS - 1)]
        for piece in range(2):
            mine = gathered.at[unit, pl.ds(half + piece * PIECE, PIECE)]
            pltpu.make_async_copy(mine, mine, core_sent.at[unit, piece]).wait()
        pltpu.make_async_copy(given.at[unit], given.at[unit], pair_sent.at[unit]).wait()
        pltpu.make_async_copy(sent, sent, scatter_sent.at[unit]).wait()

        @pl.when(section < SECTIONS - 1)
        def _():
            pltpu.make_async_copy(got.at[unit], got.at[unit], gather_sent.at[unit]).wait()

        @pl.when(section == 0)
        def _():
            pltpu.make_async_copy(sent, sent, first_sent.at[unit]).wait()

        return carry

    lax.fori_loop(0, UNITS, drain, 0)
    pltpu.make_async_copy(out_got, out_got, out_sem).wait()
    for b in range(NB):
        owner = b % HALF // 2 * 2 + b // HALF
        out[:, pl.ds(b * BLOCK, BLOCK)] = out_got[owner, pl.ds(b % 2 * 8, 8), :]
    pltpu.make_async_copy(out_got.at[pl.ds(0, 31)], out_got.at[pl.ds(0, 31)], out_sent).wait()


def body(tokens, lengths, norm_gain, gate_tiles, up_tiles, in_index, down_tiles, out_index):
    bf16 = functools.partial(pltpu.VMEM, dtype=jnp.bfloat16)
    dma = pltpu.SemaphoreType.DMA
    vmem = pl.BlockSpec(memory_space=pltpu.VMEM)
    hbm = pl.BlockSpec(memory_space=pltpu.HBM)
    rows = pl.pallas_call(
        kernel,
        out_shape=jax.ShapeDtypeStruct((8, NB * BLOCK), jnp.bfloat16),
        in_specs=[hbm] * 8,
        out_specs=vmem,
        scratch_shapes=[
            pltpu.SMEM((4,), jnp.int32),
            pltpu.SMEM((1, HB, KMAX), jnp.int32),
            pltpu.SMEM((1, HB, KMAX), jnp.int32),
            pltpu.SMEM((HB, BLOCK), jnp.int32),
            pltpu.VMEM((HB, BLOCK), jnp.int32),
            bf16((4, 2, NB * BLOCK)),
            pltpu.VMEM((1, NB * BLOCK), jnp.float32),
            bf16((HB, KMAX * BLOCK, 2 * BLOCK)),
            bf16((HB, KMAX, BLOCK, BLOCK)),
            pltpu.VMEM((HB, KMAX + 1, ROWS, BLOCK), jnp.float32),
            bf16((UNITS, NB, ROWS, BLOCK)),
            bf16((NB + 1, ROWS, BLOCK)),
            bf16((UNITS, HALF, ROWS, BLOCK)),
            pltpu.VMEM((HALF, ROWS, BLOCK), jnp.float32),
            bf16((UNITS, HALF, ROWS, BLOCK)),
            bf16((UNITS, HALF, ROWS, BLOCK)),
            bf16((UNITS, CHIPS, 2, ROWS, BLOCK)),
            bf16((UNITS, 2, ROWS, BLOCK)),
            bf16((UNITS, 2, ROWS, BLOCK)),
            bf16((32, 16, BLOCK)),
            bf16((32, 16, BLOCK)),
            bf16((32, 16, BLOCK)),
            bf16((32, 16, BLOCK)),
            dma((6,)),
            dma((3, HB)),
            dma((UNITS, 2)),
            dma((UNITS,)),
            dma((UNITS, 2)),
            dma((UNITS, 2)),
            dma((UNITS,)),
            dma((UNITS,)),
            dma((UNITS,)),
            dma((UNITS,)),
            dma((UNITS,)),
            dma,
            dma,
            dma,
            dma,
        ],
        compiler_params=pltpu.CompilerParams(
            collective_id=0, has_side_effects=True, vmem_limit_bytes=60 * 1024 * 1024
        ),
        name="relay",
    )(
        lengths,
        in_index,
        out_index,
        tokens,
        norm_gain,
        gate_tiles.reshape(HB, KMAX * BLOCK, BLOCK),
        up_tiles.reshape(HB, KMAX * BLOCK, BLOCK),
        down_tiles.reshape(HB, KMAX, BLOCK, BLOCK),
    )
    return rows.reshape(1, 4, 2, NB * BLOCK)


def solution(mesh):
    placed = (
        P(None, "shard", None),
        P(),
        P("section", None),
        P("section", "shard", None, None, None),
        P("section", "shard", None, None, None),
        P("section", "shard", None),
        P("section", "shard", None, None, None),
        P("section", "shard", None),
    )
    return jax.shard_map(
        body,
        mesh=mesh,
        in_specs=placed,
        out_specs=P("section", None, "shard", None),
        check_vma=False,
    )
```

```python
import functools

import jax
import jax.numpy as jnp
from jax import lax
from jax.experimental import pallas as pl
from jax.experimental.pallas import tpu as pltpu
from jax.sharding import PartitionSpec as P

NORM_EPS = 1e-05
LIVE = 160
ROWS = 16
UNITS = LIVE // ROWS
SIDE = 4
CHIPS = SIDE * SIDE
SECTIONS = 8
BLOCK = 128
NB = 64
HALF = NB // 2
HB = 4
PIECE = 16
KMAX = 28
LAG = 3
LEAD = 3
MESH = pl.DeviceIdType.MESH
SEND_ORDER = sorted(range(CHIPS), key=lambda step: -sum(min(d, SIDE - d) for d in divmod(step, SIDE)))


def kernel(
    lengths_in, in_index_in, out_index_in, tokens_in, gain_in, gate, up, down, out,
    lengths, in_index, out_index, inverse, inverse_rows, tokens, gain,
    gate_up, down_tiles, parts, gathered, normed, given, kept, core_got, summed, got, first, result, places,
    row_send, row_got, out_send, out_got,
    small_sem, load_sem, gather_sem, gather_sent, core_sem, core_sent, pair_sem, pair_sent,
    scatter_sem, scatter_sent, first_sent, row_sem, row_sent, out_sem, out_sent,
):
    section = lax.axis_index("section")
    shard = lax.axis_index("shard")
    chip = shard // 2
    core = shard % 2
    chip_y = chip // SIDE
    chip_x = chip % SIDE
    half = core * HALF
    other_half = HALF - half
    own = half + chip * 2
    partner = (section, chip * 2 + 1 - core)

    ys = [(chip_y + step) % SIDE * SIDE for step in range(SIDE)]
    xs = [(chip_x + step) % SIDE for step in range(SIDE)]
    chips = [y + x for y in ys for x in xs]
    peers = [there * 2 + core for there in chips]

    barrier = pltpu.get_barrier_semaphore()
    before = (section + SECTIONS - 1) % SECTIONS
    others = []
    for step in SEND_ORDER:
        pl.semaphore_signal(barrier, inc=1, device_id=(before, peers[step]), device_id_type=MESH)
        others.append(chips[step] * 2 + 1 - core)
        if step > 0:
            others.append(peers[step])
    for there in others:
        pl.semaphore_signal(barrier, inc=1, device_id=(section, there), device_id_type=MESH)

    smalls = [
        pltpu.make_async_copy(lengths_in, lengths, small_sem.at[0]),
        pltpu.make_async_copy(in_index_in, in_index, small_sem.at[1]),
        pltpu.make_async_copy(out_index_in, out_index, small_sem.at[2]),
        pltpu.make_async_copy(tokens_in, tokens, small_sem.at[3]),
        pltpu.make_async_copy(gain_in, gain, small_sem.at[4]),
    ]
    for small in smalls:
        small.start()
    loads = []
    for j in range(HB):
        loads.append(pltpu.make_async_copy(gate.at[j], gate_up.at[j, :, pl.ds(0, BLOCK)], load_sem.at[0, j]))
        loads.append(pltpu.make_async_copy(up.at[j], gate_up.at[j, :, pl.ds(BLOCK, BLOCK)], load_sem.at[1, j]))
        loads.append(pltpu.make_async_copy(down.at[j], down_tiles.at[j], load_sem.at[2, j]))
    for load in loads:
        load.start()

    for small in smalls:
        small.wait()
    offsets = [jnp.int32(0)]
    for m in range(3):
        offsets.append(offsets[-1] + lengths[m])

    def position(index):
        block = (index >> 3) & 1
        micro = (index >> 1) & 3
        row = (index >> 4) * 2 + (index & 1)
        start = jnp.full_like(index, 0)
        length = jnp.full_like(index, lengths[0])
        for m in range(1, 4):
            start = jnp.where(micro == m, offsets[m], start)
            length = jnp.where(micro == m, lengths[m], length)
        return jnp.where(row < length, start + row, -1), block

    blocks = lax.broadcasted_iota(jnp.int32, (1, BLOCK), 1)
    for j in range(HB):
        row = jnp.full((1, BLOCK), KMAX, jnp.int32)
        for k in range(KMAX):
            row = jnp.where(blocks == out_index[0, j, k], k, row)
        inverse_rows[j : j + 1, :] = row
    inverse_copy = pltpu.make_async_copy(inverse_rows, inverse, small_sem.at[5])
    inverse_copy.start()
    for j in range(HB):
        parts[j, KMAX] = jnp.zeros((ROWS, BLOCK), jnp.float32)
    normed[NB] = jnp.zeros((ROWS, BLOCK), jnp.bfloat16)

    @pl.when(section == 0)
    def _():
        for b in range(NB):
            owner = b % HALF // 2 * 2 + b // HALF
            rows = [tokens[m, :, pl.ds(b * BLOCK, BLOCK)].astype(jnp.float32) for m in range(4)]
            row_send[owner, pl.ds(b % 2 * 8, 8), :] = jnp.concatenate(rows, axis=0).astype(jnp.bfloat16)

    where, block = position(lax.broadcasted_iota(jnp.int32, (512, LIVE), 0))
    at = lax.broadcasted_iota(jnp.int32, (512, LIVE), 1)
    for b in range(2):
        places[b] = jnp.where((where == at) & (block == b), 1.0, 0.0).astype(jnp.bfloat16)

    inverse_copy.wait()
    pl.semaphore_wait(barrier, 31 + CHIPS)

    @pl.when(section == 0)
    def _():
        pltpu.make_async_copy(row_send.at[shard], row_got.at[shard], row_sem).start()

        for there in others:
            pltpu.make_async_remote_copy(
                row_send.at[there], row_got.at[shard], row_sent, row_sem, device_id=(section, there), device_id_type=MESH
            ).start()

    for load in loads:
        load.wait()

    def send_first(unit):
        pltpu.make_async_copy(first.at[unit], gathered.at[unit, pl.ds(own, 2)], gather_sem.at[unit]).start()
        for step in SEND_ORDER[:-1]:
            pltpu.make_async_remote_copy(
                first.at[unit],
                gathered.at[unit, pl.ds(own, 2)],
                first_sent.at[unit],
                gather_sem.at[unit],
                device_id=(section, peers[step]),
                device_id_type=MESH,
            ).start()

    @pl.when(section == 0)
    def _():
        where, block = position(lax.broadcasted_iota(jnp.int32, (LIVE, 512), 1))
        at = lax.broadcasted_iota(jnp.int32, (LIVE, 512), 0)
        picks = [jnp.where((where == at) & (block == b), 1.0, 0.0).astype(jnp.bfloat16) for b in range(2)]
        pltpu.make_async_copy(row_got, row_got, row_sem).wait()
        rows = row_got[...].reshape(512, BLOCK)
        for b in range(2):
            compact = jnp.dot(picks[b], rows, preferred_element_type=jnp.float32).astype(jnp.bfloat16)
            first[:, b] = compact.reshape(UNITS, ROWS, BLOCK)
        for unit in range(LEAD):
            send_first(unit)
        pltpu.make_async_copy(row_got.at[pl.ds(0, 31)], row_got.at[pl.ds(0, 31)], row_sent).wait()

    def scale(unit, start):
        total = jnp.zeros((ROWS, BLOCK), jnp.float32)
        for b in range(HALF):
            x = gathered[unit, start + b].astype(jnp.float32)
            total = total + x * x
            columns = pl.ds(pl.multiple_of((start + b) * BLOCK, BLOCK), BLOCK)
            normed[start + b] = (x * gain[0:1, columns]).astype(jnp.bfloat16)
        return total

    def arrive(unit):
        mine = gathered.at[unit, pl.ds(half, HALF)]
        pltpu.make_async_copy(mine, mine, gather_sem.at[unit]).wait()
        pltpu.make_async_remote_copy(
            mine, mine, core_sent.at[unit], core_sem.at[unit], device_id=partner, device_id_type=MESH
        ).start()

    def multiply(unit):
        total = scale(unit, half)
        theirs = gathered.at[unit, pl.ds(other_half, HALF)]
        pltpu.make_async_copy(theirs, theirs, core_sem.at[unit]).wait()
        total = total + scale(unit, other_half)
        mean = jnp.sum(total, axis=-1, keepdims=True) * (1.0 / (NB * BLOCK))
        row_scale = lax.rsqrt(mean + NORM_EPS)

        both = []
        for j in range(HB):
            picked = []
            for k in range(KMAX):
                slot = in_index[0, j, k]
                picked.append(normed[jnp.where(slot < 0, NB, slot)])
            both.append(
                jnp.dot(jnp.concatenate(picked, axis=1), gate_up[j], preferred_element_type=jnp.float32)
            )
        hidden = []
        for j in range(HB):
            gate_val = both[j][:, :BLOCK] * row_scale
            up_val = both[j][:, BLOCK:] * row_scale
            hidden.append((gate_val / (1.0 + jnp.exp(-gate_val)) * up_val).astype(jnp.bfloat16))

        for k in range(0, KMAX, 2):
            for j in range(HB):
                two = jnp.concatenate([down_tiles[j, k], down_tiles[j, k + 1]], axis=1)
                product = jnp.dot(hidden[j], two, preferred_element_type=jnp.float32)
                parts[j, k] = product[:, :BLOCK]
                parts[j, k + 1] = product[:, BLOCK:]

        def total_of(block):
            total = parts[0, inverse[0, block]]
            for j in range(1, HB):
                total = total + parts[j, inverse[j, block]]
            return total

        for piece in range(2):
            for at in range(piece * PIECE, (piece + 1) * PIECE):
                block = chips[SEND_ORDER[at // 2]] * 2 + at % 2
                given[unit, at] = total_of(other_half + block).astype(jnp.bfloat16)
            part = pl.ds(piece * PIECE, PIECE)
            pltpu.make_async_remote_copy(
                given.at[unit, part],
                core_got.at[unit, part],
                pair_sent.at[unit, piece],
                pair_sem.at[unit, piece],
                device_id=partner,
                device_id_type=MESH,
            ).start()
        for at in range(HALF):
            kept[at] = total_of(half + chips[SEND_ORDER[at // 2]] * 2 + at % 2)

    def scatter(unit):
        for piece in range(2):
            part = core_got.at[unit, pl.ds(piece * PIECE, PIECE)]
            pltpu.make_async_copy(part, part, pair_sem.at[unit, piece]).wait()
            for at in range(piece * PIECE, (piece + 1) * PIECE):
                summed[unit, at] = (kept[at] + core_got[unit, at].astype(jnp.float32)).astype(jnp.bfloat16)
            for at in range(piece * PIECE // 2, (piece + 1) * PIECE // 2):
                ours = summed.at[unit, pl.ds(at * 2, 2)]
                if at == CHIPS - 1:
                    pltpu.make_async_copy(ours, got.at[unit, chip], scatter_sem.at[unit]).start()
                else:
                    pltpu.make_async_remote_copy(
                        ours,
                        got.at[unit, chip],
                        scatter_sent.at[unit],
                        scatter_sem.at[unit],
                        device_id=(section, peers[SEND_ORDER[at]]),
                        device_id_type=MESH,
                    ).start()

    def finish(unit):
        pltpu.make_async_copy(got.at[unit], got.at[unit], scatter_sem.at[unit]).wait()
        for b in range(2):
            total = got[unit, 0, b].astype(jnp.float32)
            for c in range(1, CHIPS):
                total = total + got[unit, c, b].astype(jnp.float32)
            result[unit, b] = (gathered[unit, own + b].astype(jnp.float32) + total).astype(jnp.bfloat16)

        @pl.when(section < SECTIONS - 1)
        def _():
            for step in SEND_ORDER:
                pltpu.make_async_remote_copy(
                    result.at[unit],
                    gathered.at[unit, pl.ds(own, 2)],
                    gather_sent.at[unit],
                    gather_sem.at[unit],
                    device_id=(section + 1, peers[step]),
                    device_id_type=MESH,
                ).start()

    def turn(now, carry):
        @pl.when(now < UNITS)
        def _():
            arrive(now)

        @pl.when(now >= LAG)
        def _():
            finish(now - LAG)

        @pl.when((section == 0) & (now + LEAD < UNITS))
        def _():
            send_first(now + LEAD)

        @pl.when((now >= 1) & (now <= UNITS))
        def _():
            scatter(now - 1)

        @pl.when(now < UNITS)
        def _():
            multiply(now)

        return carry

    lax.fori_loop(0, UNITS + LAG, turn, 0)

    spread = jnp.zeros((512, BLOCK), jnp.float32)
    for b in range(2):
        spread = spread + jnp.dot(places[b], result[:, b].reshape(LIVE, BLOCK), preferred_element_type=jnp.float32)
    out_send[...] = spread.astype(jnp.bfloat16).reshape(32, 16, BLOCK)
    pltpu.make_async_copy(out_send.at[shard], out_got.at[shard], out_sem).start()

    for there in others:
        pltpu.make_async_remote_copy(
            out_send.at[there], out_got.at[shard], out_sent, out_sem, device_id=(section, there), device_id_type=MESH
        ).start()

    def drain(unit, carry):
        mine = gathered.at[unit, pl.ds(half, HALF)]
        sent = got.at[unit, pl.ds(0, CHIPS - 1)]
        pltpu.make_async_copy(mine, mine, core_sent.at[unit]).wait()
        for piece in range(2):
            part = given.at[unit, pl.ds(piece * PIECE, PIECE)]
            pltpu.make_async_copy(part, part, pair_sent.at[unit, piece]).wait()
        pltpu.make_async_copy(sent, sent, scatter_sent.at[unit]).wait()

        @pl.when(section < SECTIONS - 1)
        def _():
            pltpu.make_async_copy(got.at[unit], got.at[unit], gather_sent.at[unit]).wait()

        @pl.when(section == 0)
        def _():
            pltpu.make_async_copy(sent, sent, first_sent.at[unit]).wait()

        return carry

    lax.fori_loop(0, UNITS, drain, 0)
    pltpu.make_async_copy(out_got, out_got, out_sem).wait()
    for b in range(NB):
        owner = b % HALF // 2 * 2 + b // HALF
        out[:, pl.ds(b * BLOCK, BLOCK)] = out_got[owner, pl.ds(b % 2 * 8, 8), :]
    pltpu.make_async_copy(out_got.at[pl.ds(0, 31)], out_got.at[pl.ds(0, 31)], out_sent).wait()


def body(tokens, lengths, norm_gain, gate_tiles, up_tiles, in_index, down_tiles, out_index):
    bf16 = functools.partial(pltpu.VMEM, dtype=jnp.bfloat16)
    dma = pltpu.SemaphoreType.DMA
    vmem = pl.BlockSpec(memory_space=pltpu.VMEM)
    hbm = pl.BlockSpec(memory_space=pltpu.HBM)
    rows = pl.pallas_call(
        kernel,
        out_shape=jax.ShapeDtypeStruct((8, NB * BLOCK), jnp.bfloat16),
        in_specs=[hbm] * 8,
        out_specs=vmem,
        scratch_shapes=[
            pltpu.SMEM((4,), jnp.int32),
            pltpu.SMEM((1, HB, KMAX), jnp.int32),
            pltpu.SMEM((1, HB, KMAX), jnp.int32),
            pltpu.SMEM((HB, BLOCK), jnp.int32),
            pltpu.VMEM((HB, BLOCK), jnp.int32),
            bf16((4, 2, NB * BLOCK)),
            pltpu.VMEM((1, NB * BLOCK), jnp.float32),
            bf16((HB, KMAX * BLOCK, 2 * BLOCK)),
            bf16((HB, KMAX, BLOCK, BLOCK)),
            pltpu.VMEM((HB, KMAX + 1, ROWS, BLOCK), jnp.float32),
            bf16((UNITS, NB, ROWS, BLOCK)),
            bf16((NB + 1, ROWS, BLOCK)),
            bf16((UNITS, HALF, ROWS, BLOCK)),
            pltpu.VMEM((HALF, ROWS, BLOCK), jnp.float32),
            bf16((UNITS, HALF, ROWS, BLOCK)),
            bf16((UNITS, HALF, ROWS, BLOCK)),
            bf16((UNITS, CHIPS, 2, ROWS, BLOCK)),
            bf16((UNITS, 2, ROWS, BLOCK)),
            bf16((UNITS, 2, ROWS, BLOCK)),
            bf16((2, 512, LIVE)),
            bf16((32, 16, BLOCK)),
            bf16((32, 16, BLOCK)),
            bf16((32, 16, BLOCK)),
            bf16((32, 16, BLOCK)),
            dma((6,)),
            dma((3, HB)),
            dma((UNITS,)),
            dma((UNITS,)),
            dma((UNITS,)),
            dma((UNITS,)),
            dma((UNITS, 2)),
            dma((UNITS, 2)),
            dma((UNITS,)),
            dma((UNITS,)),
            dma((UNITS,)),
            dma,
            dma,
            dma,
            dma,
        ],
        compiler_params=pltpu.CompilerParams(
            collective_id=0, has_side_effects=True, vmem_limit_bytes=60 * 1024 * 1024
        ),
        name="relay",
    )(
        lengths,
        in_index,
        out_index,
        tokens,
        norm_gain,
        gate_tiles.reshape(HB, KMAX * BLOCK, BLOCK),
        up_tiles.reshape(HB, KMAX * BLOCK, BLOCK),
        down_tiles.reshape(HB, KMAX, BLOCK, BLOCK),
    )
    return rows.reshape(1, 4, 2, NB * BLOCK)


def solution(mesh):
    placed = (
        P(None, "shard", None),
        P(),
        P("section", None),
        P("section", "shard", None, None, None),
        P("section", "shard", None, None, None),
        P("section", "shard", None),
        P("section", "shard", None, None, None),
        P("section", "shard", None),
    )
    return jax.shard_map(
        body,
        mesh=mesh,
        in_specs=placed,
        out_specs=P("section", None, "shard", None),
        check_vma=False,
    )
```
